32 devices in a mesh: rep: 1, exp: 32 (over z, y, x, core).
Axes of the slice: x: 2, y: 2, z: 4, core: 2. Of those that a mesh axis runs over, the one named last changes fastest.
Arguments:
- hidden: bfloat16 [512, 7168], P(('rep', 'exp')), may hold values from -6 to 6
- expert_ids: int32 [512, 8], P(('rep', 'exp')), may hold values from 0 to 15, all different within a row; in each aligned block of 16 rows (0 to 15, 16 to 31, ...) at most 10 rows name the same one
- router: bfloat16 [7168, 16], replicated, may hold values from -0.0625 to 0.0625
- gate_up: bfloat16 [32, 512, 2, 7168], P('exp', 'rep'), may hold values from -0.0625 to 0.0625
- down_weight: bfloat16 [32, 512, 7168], P('exp', 'rep'), may hold values from -0.1875 to 0.1875
- query_latent: bfloat16 [512, 64, 512], P(('rep', 'exp')), may hold values from -110 to 110
- query_rope: bfloat16 [512, 64, 64], P(('rep', 'exp')), may hold values from -6 to 6
- cache_latent: bfloat16 [512, 256, 512], P(('rep', 'exp')), may hold values from -8 to 8
- cache_rope: bfloat16 [512, 64, 256], P(('rep', 'exp')), may hold values from -5 to 5
- lengths: int32 [512], P(('rep', 'exp')), may hold values from 32 to 256, as said below
Outputs:
- moe_out: bfloat16 [512, 7168], P(('rep', 'exp'))
- attn_latent: bfloat16 [512, 64, 512], P(('rep', 'exp'))
The draws below stay inside these ranges and needn't reach their ends.
Inputs may be any that keep to these rules, and one draw needn't show every extreme that they name: `expert_ids`: in every aligned block of 16 rows no expert is named by more than 10 pairs, a bound that some block reaches. `lengths`: some row has length 256.
All inputs are finite; a program needn't handle non-finite values.
Results may differ from the reference program's by a relative error of at most 0.015.
Values may be sent and summed in bfloat16 or wider, within the bound.
A program may use at most 128 MiB of HBM per device.

```python
import math
from functools import partial
import jax
import jax.numpy as jnp
import numpy as np
from jax import lax

D = 7168
EXPERT_HIDDEN = 1024
NH = 64
KVL = 512
ROPE = 64
NOPE = 128
TOP = 8
ROWS = 16
LEN = 256
HID_DEV = 512
EXPERTS = 16
CAP = 10
TOKENS = 512
N_REP = 1
N_EXP = 32


def pair_keys(key):
    first_keys = jax.random.truncated_normal(jax.random.fold_in(key, 21), -5.0, 5.0, (TOKENS, 2, KVL), jnp.float32)
    rope_keys = jax.random.truncated_normal(jax.random.fold_in(key, 22), -5.0, 5.0, (TOKENS, ROPE, 2), jnp.float32)
    return (first_keys, rope_keys)


def draw_cache_latent(key, part):
    first_keys, rope_keys = pair_keys(key)
    remaining = jax.random.truncated_normal(jax.random.fold_in(key, 23), -5.0, 5.0, (TOKENS, LEN - 2, KVL), jnp.float32)
    return jnp.concatenate((first_keys, remaining), axis=1).astype(jnp.bfloat16)


def draw_cache_rope(key, part):
    first_keys, rope_keys = pair_keys(key)
    remaining = jax.random.truncated_normal(jax.random.fold_in(key, 24), -5.0, 5.0, (TOKENS, ROPE, LEN - 2), jnp.float32)
    return jnp.concatenate((rope_keys, remaining), axis=2).astype(jnp.bfloat16)


def draw_query_latent(key, part):
    base_draw = jax.random.truncated_normal(jax.random.fold_in(key, 25), -5.0, 5.0, (TOKENS, NH, KVL), jnp.float32)
    return base_draw.astype(jnp.bfloat16)


def draw_query_rope(key, part):
    base_draw = jax.random.truncated_normal(jax.random.fold_in(key, 26), -5.0, 5.0, (TOKENS, NH, ROPE), jnp.float32)
    return base_draw.astype(jnp.bfloat16)


def draw_lengths(key, part):
    drawn = jax.random.randint(jax.random.fold_in(key, 31), (TOKENS,), max(2, LEN // 8), LEN + 1, dtype=jnp.int32)
    return jnp.where(jnp.arange(TOKENS, dtype=jnp.int32) == 0, LEN, drawn).astype(jnp.int32)


def block_scale(stream_key, shape, shards, low, top_value):
    gain, own = 1.0, jax.random.fold_in(stream_key, 6)
    for axis_at, shards_of in shards:
        draws = jnp.exp(jax.random.uniform(jax.random.fold_in(own, axis_at), (shards_of,), jnp.float32, low / len(shards), top_value / len(shards)))
        gain = gain * jnp.repeat(draws, shape[axis_at] // shards_of).reshape([-1 if axis == axis_at else 1 for axis in range(len(shape))])
    return gain


def deal_out(stream_key, own, number, rows, amount, top, limit, skew):
    sequence = jax.random.permutation(stream_key, amount)
    crowded, common = load_shares(amount, rows * top, limit, skew, True), load_shares(amount, rows * top, limit, skew, False)
    places = jnp.arange(amount)

    def named(sizes, offset_by):
        used = int((sizes > 0).sum())
        fixed = max(1, used // 4)
        passed = fixed + (places - fixed + offset_by * (used - fixed)) % max(1, amount - fixed)
        return jnp.zeros((amount,), jnp.int32).at[sequence[jnp.where(places < fixed, places, passed)]].set(jnp.asarray(sizes, jnp.int32))

    sizes = jnp.where(number % 4 == 0, named(crowded, number // 4), named(common, number - number // 4 - 1))
    mixed = jax.random.permutation(jax.random.fold_in(own, 3), amount)
    giver, sink = mixed[0:amount // 2 * 2:2], mixed[1:amount // 2 * 2:2]
    slack = jnp.minimum(sizes[giver] - 1, limit - sizes[sink]) // 2
    slack = jnp.where((giver == sequence[0]) | (sink == sequence[0]) | (sizes[sink] == 0), 0, jnp.maximum(slack, 0))
    passed = jax.random.randint(jax.random.fold_in(own, 4), (amount // 2,), 0, 1 << 20) % (slack + 1)
    sizes = sizes.at[giver].add(-passed).at[sink].add(passed)
    labels = jnp.searchsorted(jnp.cumsum(sizes), jnp.arange(rows * top), side="right").astype(jnp.int32)
    listing = labels.reshape(top, rows).T
    listing = listing[jax.random.permutation(jax.random.fold_in(own, 1), rows)]
    offset_by = jax.random.randint(jax.random.fold_in(own, 2), (rows, 1), 0, top)
    return jnp.take_along_axis(listing, (jnp.arange(top)[None, :] + offset_by) % top, axis=1)


def load_shares(amount, total, limit, lean, full):
    portions = [(1 << 20) // math.isqrt(rank ** lean) + 1 for rank in range(1, amount + 1)]
    largest = limit if full else min(limit, max(-(-total // amount), total * portions[0] // sum(portions)))
    least = 1 if total - largest >= amount - 1 else 0
    holding, surplus = [largest] + [least] * (amount - 1), total - largest - least * (amount - 1)
    while surplus > 0:
        movable = [i for i in range(1, amount) if holding[i] < largest] or [i for i in range(1, amount) if holding[i] < limit]
        whole, left = sum([portions[i] for i in movable]), surplus
        for i in movable:
            extra = min(limit - holding[i], max(1, left * portions[i] // whole), surplus)
            holding[i] = holding[i] + extra
            surplus = surplus - extra
    return np.array(holding)


def gaussian(own_key, extent, deviation, limit, split=(), kind=jnp.bfloat16):
    gain = block_scale(own_key, extent, split, -0.22, 0.18) if split else 1.0
    values = jax.random.normal(own_key, extent, jnp.float32) * deviation * gain
    return jnp.minimum(jnp.maximum(values, -limit), limit).astype(kind)


def setup_inputs(seed: int = 0) -> dict:
    streams_of = jax.random.split(jax.random.key(seed), 11)
    hidden = gaussian(streams_of[0], (TOKENS, D), 1.0, 6.0, ((0, 32),))
    expert_ids_keys = jax.random.split(jax.random.fold_in(streams_of[1], 1), TOKENS // ROWS)
    expert_ids_turns = jax.random.permutation(jax.random.fold_in(streams_of[1], 3), TOKENS // ROWS)
    expert_ids = jax.vmap(lambda own, number: deal_out(jax.random.fold_in(streams_of[1], 2), own, number, ROWS, EXPERTS, TOP, CAP, 2))(expert_ids_keys, expert_ids_turns).reshape((TOKENS, TOP))
    router = gaussian(streams_of[2], (D, EXPERTS), D ** -0.5, 0.0625)
    gate_up = gaussian(streams_of[3], (N_EXP, HID_DEV, 2, D), D ** -0.5, 0.0625, ((0, 32),))
    down_weight = gaussian(streams_of[4], (N_EXP, HID_DEV, D), EXPERT_HIDDEN ** -0.5, 0.1875, ((0, 32),))
    query_latent = draw_query_latent(jax.random.fold_in(streams_of[10], 71), 0)
    query_rope = draw_query_rope(jax.random.fold_in(streams_of[10], 71), 0)
    cache_latent = draw_cache_latent(jax.random.fold_in(streams_of[10], 71), 0)
    cache_rope = draw_cache_rope(jax.random.fold_in(streams_of[10], 71), 0)
    lengths = draw_lengths(jax.random.fold_in(streams_of[10], 71), 0)
    return dict(hidden=hidden, expert_ids=expert_ids, router=router, gate_up=gate_up, down_weight=down_weight, query_latent=query_latent, query_rope=query_rope, cache_latent=cache_latent, cache_rope=cache_rope, lengths=lengths)


route_scale = 2.827

def slot_table(expert_ids, experts, capacity):
    flat_ids = expert_ids.reshape(-1).astype(jnp.int32)
    onehot = (flat_ids[:, None] == jnp.arange(experts, dtype=jnp.int32)[None, :]).astype(jnp.int32)
    earlier = (jnp.cumsum(onehot, axis=0) - onehot).astype(jnp.int32)
    slot_rank = lax.optimization_barrier(jnp.sum(earlier * onehot, axis=1)).astype(jnp.int32)
    return (flat_ids * capacity + slot_rank).astype(jnp.int32)

def bucket_rows(rows_in, flat_slot, experts, capacity):
    row_total = rows_in.shape[0]
    pair_total = flat_slot.shape[0]
    slot_matrix = (jnp.arange(experts * capacity, dtype=jnp.int32)[:, None] == flat_slot[None, :]).astype(jnp.float32)
    slot_matrix = lax.optimization_barrier(jnp.sum(slot_matrix.reshape(experts * capacity, row_total, pair_total // row_total), axis=2))
    return jnp.dot(slot_matrix.astype(jnp.bfloat16), rows_in, preferred_element_type=jnp.float32).astype(jnp.bfloat16)

def partial_output(rows_in, gate_up, down_weight):
    dims = (((1,), (1,)), ((), ()))
    gate_value = lax.dot_general(rows_in, gate_up[:, 0, :], dims, preferred_element_type=jnp.float32)
    up_value = lax.dot_general(rows_in, gate_up[:, 1, :], dims, preferred_element_type=jnp.float32)
    activated = (jax.nn.silu(gate_value) * up_value).astype(jnp.bfloat16)
    return jnp.dot(activated, down_weight, preferred_element_type=jnp.float32)

def attend(query_latent, query_rope, cache_latent, cache_rope, row_lengths):
    score_scale = 1.0 / math.sqrt(NOPE + ROPE)
    scores = jnp.einsum('rhc,rlc->rhl', query_latent.astype(jnp.float32), cache_latent.astype(jnp.float32))
    scores = scores + jnp.einsum('rhp,rpl->rhl', query_rope.astype(jnp.float32), cache_rope.astype(jnp.float32))
    scores = scores * score_scale
    valid_mask = jnp.arange(cache_latent.shape[1], dtype=jnp.int32)[None, None, :] < row_lengths[:, None, None]
    scores = jnp.where(valid_mask, scores, -1e+30)
    row_max = lax.optimization_barrier(jnp.max(scores, axis=2, keepdims=True))
    weights_raw = jnp.where(valid_mask, jnp.exp(scores - row_max), 0.0)
    attn_probs = (weights_raw / lax.optimization_barrier(jnp.sum(weights_raw, axis=2, keepdims=True))).astype(jnp.bfloat16)
    output = jnp.einsum('rhl,rlc->rhc', attn_probs.astype(jnp.float32), cache_latent.astype(jnp.float32))
    return output.astype(jnp.bfloat16)

def pick_rows(slot_matrix, row_index):
    return jnp.take(slot_matrix, row_index, axis=0)

def reference(hidden, expert_ids, router, gate_up, down_weight, query_latent, query_rope, cache_latent, cache_rope, lengths):
    devices = N_REP * N_EXP
    logits = jnp.dot(hidden, router, preferred_element_type=jnp.float32)
    picked = jnp.take_along_axis(logits, expert_ids, axis=1)
    sigmoid_scores = jax.nn.sigmoid(picked)
    mixing = sigmoid_scores / lax.optimization_barrier(jnp.sum(sigmoid_scores, axis=1, keepdims=True)) * route_scale
    id_blocks = expert_ids.reshape(devices, ROWS * TOP)
    slot_blocks = jax.vmap(partial(slot_table, experts=EXPERTS, capacity=CAP))(id_blocks)
    hidden_blocks = hidden.reshape(devices, ROWS, D)
    buckets = jax.vmap(partial(bucket_rows, experts=EXPERTS, capacity=CAP))(hidden_blocks, slot_blocks)
    buckets = buckets.reshape(devices, EXPERTS, CAP, D).transpose(1, 0, 2, 3).reshape(EXPERTS, devices * CAP, D)
    pair_gate_up = gate_up.reshape(EXPERTS, 2, HID_DEV, 2, D)
    pair_down = down_weight.reshape(EXPERTS, 2, HID_DEV, D)

    def one_expert(member_items):
        rows_in, expert_gate_up, expert_down = member_items
        front_part = partial_output(rows_in, expert_gate_up[0], expert_down[0]).astype(jnp.bfloat16)
        back_part = partial_output(rows_in, expert_gate_up[1], expert_down[1]).astype(jnp.bfloat16)
        return (front_part.astype(jnp.float32) + back_part.astype(jnp.float32)).astype(jnp.bfloat16)
    results = lax.map(one_expert, (buckets, pair_gate_up, pair_down))
    results = results.reshape(EXPERTS, devices, CAP, D).transpose(1, 0, 2, 3).reshape(devices, EXPERTS * CAP, D)
    chosen = jax.vmap(pick_rows)(results, slot_blocks).reshape(hidden.shape[0], TOP, D)
    moe_out = lax.optimization_barrier(jnp.sum(chosen.astype(jnp.float32) * mixing[:, :, None], axis=1)).astype(jnp.bfloat16)

    def attend_block(member_items):
        return attend(*member_items)
    attn_latent = lax.map(attend_block, (query_latent.reshape(devices, ROWS, NH, KVL), query_rope.reshape(devices, ROWS, NH, ROPE), cache_latent.reshape(devices, ROWS, LEN, KVL), cache_rope.reshape(devices, ROWS, ROPE, LEN), lengths.reshape(devices, ROWS))).reshape(hidden.shape[0], NH, KVL)
    return (moe_out, attn_latent)
```

```python
import math

import jax
import jax.numpy as jnp
from jax import lax
from jax.sharding import PartitionSpec as P

ROPE = 64
NOPE = 128


route_scale = 2.827


def partial_output(rows_in, gate_up, down_weight):
    dims = (((1,), (1,)), ((), ()))
    gate_value = lax.dot_general(
        rows_in, gate_up[:, 0, :], dims, preferred_element_type=jnp.float32
    )
    up_value = lax.dot_general(rows_in, gate_up[:, 1, :], dims, preferred_element_type=jnp.float32)
    activated = (jax.nn.silu(gate_value) * up_value).astype(jnp.bfloat16)
    return jnp.dot(activated, down_weight, preferred_element_type=jnp.float32)


def attend(query_latent, query_rope, cache_latent, cache_rope, row_lengths):
    score_scale = 1.0 / math.sqrt(NOPE + ROPE)
    scores = jnp.einsum(
        "rhc,rlc->rhl", query_latent, cache_latent, preferred_element_type=jnp.float32
    )
    scores = scores + jnp.einsum(
        "rhp,rpl->rhl", query_rope, cache_rope, preferred_element_type=jnp.float32
    )
    scores = scores * score_scale
    valid_mask = (
        jnp.arange(cache_latent.shape[1], dtype=jnp.int32)[None, None, :]
        < row_lengths[:, None, None]
    )
    scores = jnp.where(valid_mask, scores, -1e30)
    row_max = jnp.max(scores, axis=2, keepdims=True)
    weights_raw = jnp.where(valid_mask, jnp.exp(scores - row_max), 0.0)
    attn_probs = (weights_raw / jnp.sum(weights_raw, axis=2, keepdims=True)).astype(jnp.bfloat16)
    output = jnp.einsum(
        "rhl,rlc->rhc", attn_probs, cache_latent, preferred_element_type=jnp.float32
    )
    return output.astype(jnp.bfloat16)


def on_device(
    hidden,
    expert_ids,
    router,
    gate_up,
    down_weight,
    query_latent,
    query_rope,
    cache_latent,
    cache_rope,
    lengths,
):
    groups = lax.axis_size("exp")
    experts = groups // 2
    full_gate_up, full_down = (
        lax.all_gather(gate_up, "rep", axis=1, tiled=True),
        lax.all_gather(down_weight, "rep", axis=1, tiled=True),
    )
    slice_gate_up = full_gate_up[0]
    slice_down = full_down[0]
    logits = jnp.dot(hidden, router, preferred_element_type=jnp.float32)
    onehot = (expert_ids[:, :, None] == jnp.arange(experts, dtype=jnp.int32)[None, None, :]).astype(
        jnp.float32
    )
    picked = jnp.sum(onehot * logits[:, None, :], axis=2)
    sigmoid_scores = jax.nn.sigmoid(picked)
    mixing = sigmoid_scores / jnp.sum(sigmoid_scores, axis=1, keepdims=True) * route_scale
    dense_mixing = jnp.sum(onehot * mixing[:, :, None], axis=1)
    all_hidden = lax.all_gather(hidden, "exp", axis=0, tiled=True)
    all_mixing = lax.all_gather(dense_mixing, "exp", axis=0, tiled=True)
    own_expert = lax.axis_index("exp") // 2
    own_mixing = jnp.sum(
        jnp.where(jnp.arange(experts)[None, :] == own_expert, all_mixing, 0.0),
        axis=1,
        keepdims=True,
    )
    weighted = (partial_output(all_hidden, slice_gate_up, slice_down) * own_mixing).astype(
        jnp.bfloat16
    )
    moe_out = lax.psum_scatter(weighted, "exp", scatter_dimension=0, tiled=True)
    attn_latent = attend(query_latent, query_rope, cache_latent, cache_rope, lengths)
    return (moe_out, attn_latent)


def solution(mesh):
    return jax.shard_map(
        on_device,
        mesh=mesh,
        in_specs=(
            P(("rep", "exp"), None),
            P(("rep", "exp"), None),
            P(),
            P("exp", "rep", None, None),
            P("exp", "rep", None),
            P(("rep", "exp"), None, None),
            P(("rep", "exp"), None, None),
            P(("rep", "exp"), None, None),
            P(("rep", "exp"), None, None),
            P(("rep", "exp")),
        ),
        out_specs=(P(("rep", "exp"), None), P(("rep", "exp"), None, None)),
        check_vma=False,
    )
```

```python
import math

import jax
import jax.numpy as jnp
from jax import lax
from jax.experimental import pallas as pl
from jax.experimental.pallas import tpu as pltpu
from jax.sharding import PartitionSpec as P

ROPE = 64
NOPE = 128


route_scale = 2.827


EXTRA = 128


def other_z(z, dz):
    return (z, z + 1 - 2 * (z % 2), z + 2 - 4 * (z // 2), 3 - z)[dz]


def expert_kernel(
    own_ref,
    gate_up_hbm,
    down_hbm,
    out_ref,
    rows_ref,
    gate_up_ref,
    down_ref,
    part_ref,
    from_core,
    from_q,
    from_p,
    from_z,
    gate_acc,
    up_acc,
    weight_sem,
    ag_send,
    ag_recv,
    rs_send,
    rs_recv,
):
    width = down_ref.shape[1]
    tile = 1024
    experts = 16
    me = lax.axis_index("exp")
    core, x, y, z = me % 2, (me // 2) % 2, (me // 4) % 2, me // 8
    p_step, q_step = 4 - 2 * core, 2 + 2 * core
    p_at = y * (1 - core) + x * core
    q_at = x * (1 - core) + y * core

    def device(zz, p, q, c):
        return 8 * zz + p_step * p + q_step * q + c

    sibling = device(z, p_at, q_at, 1 - core)
    p_near = device(z, 1 - p_at, q_at, core)
    q_near = device(z, p_at, 1 - q_at, core)
    z_near = [device(other_z(z, dz), p_at, q_at, core) for dz in range(4)]

    barrier = pltpu.get_barrier_semaphore()
    for partner in (sibling, p_near, q_near, *z_near[1:]):
        pl.semaphore_signal(
            barrier, inc=1, device_id={"exp": partner}, device_id_type=pl.DeviceIdType.MESH
        )
    gate_up_copy = pltpu.make_async_copy(gate_up_hbm, gate_up_ref, weight_sem.at[0])
    down_copy = pltpu.make_async_copy(down_hbm, down_ref, weight_sem.at[1])
    gate_up_copy.start()
    down_copy.start()
    rows_ref[me] = own_ref[...]
    pl.semaphore_wait(barrier, 6)

    sent = []

    def remote(src, dst, send, recv, target):
        return pltpu.make_async_remote_copy(
            src_ref=src,
            dst_ref=dst,
            send_sem=send,
            recv_sem=recv,
            device_id={"exp": target},
            device_id_type=pl.DeviceIdType.MESH,
        )

    ag_count = [0]

    def give(block, target):
        copy = remote(
            rows_ref.at[block],
            rows_ref.at[block],
            ag_send.at[ag_count[0]],
            ag_recv.at[block],
            target,
        )
        ag_count[0] += 1
        copy.start()
        sent.append(copy)

    def take(block):
        remote(
            rows_ref.at[block], rows_ref.at[block], ag_send.at[0], ag_recv.at[block], sibling
        ).wait_recv()

    def gather_first(dz):
        zz = other_z(z, dz)
        block = device(zz, p_at, q_at, core)
        if dz == 0:
            for far in (1, 2, 3):
                give(block, z_near[far])
        else:
            take(block)
        give(block, q_near)
        give(block, p_near)
        give(block, sibling)

    def gather_second(dz):
        zz = other_z(z, dz)
        block = device(zz, 1 - p_at, q_at, core)
        take(block)
        give(block, q_near)
        give(block, sibling)

    def gather_last(dz):
        zz = other_z(z, dz)
        for p in (p_at, 1 - p_at):
            block = device(zz, p, 1 - q_at, core)
            take(block)
            give(block, sibling)
        for p in (0, 1):
            for q in (0, 1):
                take(device(zz, p, q, 1 - core))

    rs_count = [0]

    def hand_over(block, slots, slot, recv, target):
        copy = remote(
            part_ref.at[block], slots.at[slot], rs_send.at[rs_count[0]], rs_recv.at[recv], target
        )
        rs_count[0] += 1
        copy.start()
        sent.append(copy)

    def receive(slots, slot, recv):
        remote(
            slots.at[slot], slots.at[slot], rs_send.at[0], rs_recv.at[recv], sibling
        ).wait_recv()

    def add(block, slots, slot):
        total = part_ref[block].astype(jnp.float32) + slots[slot].astype(jnp.float32)
        part_ref[block] = total.astype(jnp.bfloat16)

    def compute(dz):
        zz = other_z(z, dz)
        gate_acc[...] = jnp.zeros_like(gate_acc)
        up_acc[...] = jnp.zeros_like(up_acc)
        dims = (((1,), (1,)), ((), ()))
        planes = pl.ds(8 * zz, 8)

        @pl.loop(0, width // tile)
        def _(step):
            columns = pl.ds(pl.multiple_of(step * tile, tile), tile)
            rows = rows_ref[planes, :, columns].reshape(128, tile)
            gate_acc[...] += lax.dot_general(
                rows, gate_up_ref[0, :, columns], dims, preferred_element_type=jnp.float32
            )
            up_acc[...] += lax.dot_general(
                rows, gate_up_ref[1, :, columns], dims, preferred_element_type=jnp.float32
            )

        gate = gate_acc[...]
        act = (gate / (1.0 + jnp.exp(-gate)) * up_acc[...]).astype(jnp.bfloat16)
        extra = rows_ref[planes, :, width:].reshape(128, EXTRA).astype(jnp.float32)
        lane = lax.broadcasted_iota(jnp.int32, (128, EXTRA), 1)
        own = (lane == me // 2) | (lane == experts + me // 2)
        mixing = jnp.sum(jnp.where(own, extra, 0.0), axis=1, keepdims=True)

        if dz == 0:
            down_copy.wait()

        @pl.loop(0, width // tile)
        def _(step):
            columns = pl.ds(pl.multiple_of(step * tile, tile), tile)
            result = jnp.dot(act, down_ref[:, columns], preferred_element_type=jnp.float32)
            part_ref[planes, :, columns] = (
                (result * mixing).astype(jnp.bfloat16).reshape(8, 16, tile)
            )

        for yy in (0, 1):
            for xx in (0, 1):
                block = 8 * zz + 4 * yy + 2 * xx + 1 - core
                slot = 4 * dz + 2 * yy + xx
                hand_over(block, from_core, slot, slot, sibling)

    def sum_cores(dz):
        zz = other_z(z, dz)
        for q in (1 - q_at, q_at):
            for i, p in enumerate((1 - p_at, p_at)):
                slot = 4 * dz + (p_step // 2) * p + (q_step // 2) * q
                block = device(zz, p, q, core)
                receive(from_core, slot, slot)
                add(block, from_core, slot)
                if q is not q_at:
                    hand_over(block, from_q, 2 * dz + i, 16 + 2 * dz + i, q_near)

    def sum_q(dz):
        zz = other_z(z, dz)
        for i, p in enumerate((1 - p_at, p_at)):
            block = device(zz, p, q_at, core)
            receive(from_q, 2 * dz + i, 16 + 2 * dz + i)
            add(block, from_q, 2 * dz + i)
            if i == 0:
                hand_over(block, from_p, dz, 24 + dz, p_near)

    def sum_p(dz):
        block = z_near[dz]
        receive(from_p, dz, 24 + dz)
        add(block, from_p, dz)
        if dz:
            hand_over(block, from_z, dz - 1, 27 + dz, z_near[dz])

    gather_first(0)
    gather_first(1)
    gather_second(0)
    gather_first(2)
    gather_second(1)
    gather_last(0)
    gate_up_copy.wait()
    compute(0)
    gather_first(3)
    gather_second(2)
    gather_last(1)
    sum_cores(0)
    compute(1)
    gather_second(3)
    gather_last(2)
    sum_cores(1)
    sum_q(0)
    compute(2)
    gather_last(3)
    sum_cores(2)
    sum_q(1)
    sum_p(0)
    compute(3)
    sum_cores(3)
    sum_q(2)
    sum_p(1)
    sum_q(3)
    sum_p(2)
    sum_p(3)
    total = part_ref[me].astype(jnp.float32)
    for dz in (1, 2, 3):
        receive(from_z, dz - 1, 27 + dz)
        total = total + from_z[dz - 1].astype(jnp.float32)
    out_ref[...] = total.astype(jnp.bfloat16)
    for copy in sent:
        copy.wait_send()


def experts_layer(own, gate_up, down):
    hidden_dev, width = down.shape
    rows_dev = own.shape[0]
    groups = lax.axis_size("exp")
    block = (rows_dev, width)
    flops = 2 * groups * rows_dev * width * hidden_dev * 3
    return pl.pallas_call(
        expert_kernel,
        out_shape=jax.ShapeDtypeStruct(block, jnp.bfloat16),
        in_specs=[
            pl.BlockSpec(memory_space=pltpu.VMEM),
            pl.BlockSpec(memory_space=pl.ANY),
            pl.BlockSpec(memory_space=pl.ANY),
        ],
        out_specs=pl.BlockSpec(memory_space=pltpu.VMEM),
        scratch_shapes=[
            pltpu.VMEM((groups, rows_dev, width + EXTRA), jnp.bfloat16),
            pltpu.VMEM((2, hidden_dev, width), jnp.bfloat16),
            pltpu.VMEM((hidden_dev, width), jnp.bfloat16),
            pltpu.VMEM((groups, *block), jnp.bfloat16),
            pltpu.VMEM((16, *block), jnp.bfloat16),
            pltpu.VMEM((8, *block), jnp.bfloat16),
            pltpu.VMEM((4, *block), jnp.bfloat16),
            pltpu.VMEM((3, *block), jnp.bfloat16),
            pltpu.VMEM((8 * rows_dev, hidden_dev), jnp.float32),
            pltpu.VMEM((8 * rows_dev, hidden_dev), jnp.float32),
            pltpu.SemaphoreType.DMA((2,)),
            pltpu.SemaphoreType.DMA((31,)),
            pltpu.SemaphoreType.DMA((groups,)),
            pltpu.SemaphoreType.DMA((31,)),
            pltpu.SemaphoreType.DMA((31,)),
        ],
        compiler_params=pltpu.CompilerParams(
            collective_id=0, has_side_effects=True, vmem_limit_bytes=56 * 2**20
        ),
        cost_estimate=pl.CostEstimate(
            flops=flops, bytes_accessed=6 * hidden_dev * width, transcendentals=0
        ),
    )(own, gate_up, down)


def attend(query_latent, query_rope, cache_latent, cache_rope, row_lengths):
    score_scale = 1.0 / math.sqrt(NOPE + ROPE)
    scores = jnp.einsum(
        "rhc,rlc->rhl", query_latent, cache_latent, preferred_element_type=jnp.float32
    )
    scores = scores + jnp.einsum(
        "rhp,rpl->rhl", query_rope, cache_rope, preferred_element_type=jnp.float32
    )
    scores = scores * score_scale
    valid_mask = (
        jnp.arange(cache_latent.shape[1], dtype=jnp.int32)[None, None, :]
        < row_lengths[:, None, None]
    )
    scores = jnp.where(valid_mask, scores, -1e30)
    row_max = jnp.max(scores, axis=2, keepdims=True)
    weights_raw = jnp.where(valid_mask, jnp.exp(scores - row_max), 0.0)
    attn_probs = (weights_raw / jnp.sum(weights_raw, axis=2, keepdims=True)).astype(jnp.bfloat16)
    output = jnp.einsum(
        "rhl,rlc->rhc", attn_probs, cache_latent, preferred_element_type=jnp.float32
    )
    return output.astype(jnp.bfloat16)


def on_device(
    hidden,
    expert_ids,
    router,
    gate_up,
    down_weight,
    query_latent,
    query_rope,
    cache_latent,
    cache_rope,
    lengths,
):
    groups = lax.axis_size("exp")
    experts = groups // 2
    full_gate_up, full_down = (
        lax.all_gather(gate_up, "rep", axis=1, tiled=True),
        lax.all_gather(down_weight, "rep", axis=1, tiled=True),
    )
    slice_gate_up = full_gate_up[0]
    slice_down = full_down[0]
    logits = jnp.dot(hidden, router, preferred_element_type=jnp.float32)
    onehot = (expert_ids[:, :, None] == jnp.arange(experts, dtype=jnp.int32)[None, None, :]).astype(
        jnp.float32
    )
    picked = jnp.sum(onehot * logits[:, None, :], axis=2)
    sigmoid_scores = jax.nn.sigmoid(picked)
    mixing = sigmoid_scores / jnp.sum(sigmoid_scores, axis=1, keepdims=True) * route_scale
    dense_mixing = jnp.sum(onehot * mixing[:, :, None], axis=1)
    high = lax.reduce_precision(dense_mixing, 8, 7)
    extra = jnp.concatenate((high, dense_mixing - high), axis=1)
    extra = jnp.pad(extra, ((0, 0), (0, EXTRA - extra.shape[1]))).astype(jnp.bfloat16)
    own = jnp.concatenate((hidden, extra), axis=1)
    moe_out = experts_layer(own, slice_gate_up.transpose(1, 0, 2), slice_down)
    attn_latent = attend(query_latent, query_rope, cache_latent, cache_rope, lengths)
    return (moe_out, attn_latent)


def solution(mesh):
    return jax.shard_map(
        on_device,
        mesh=mesh,
        in_specs=(
            P(("rep", "exp"), None),
            P(("rep", "exp"), None),
            P(),
            P("exp", "rep", None, None),
            P("exp", "rep", None),
            P(("rep", "exp"), None, None),
            P(("rep", "exp"), None, None),
            P(("rep", "exp"), None, None),
            P(("rep", "exp"), None, None),
            P(("rep", "exp")),
        ),
        out_specs=(P(("rep", "exp"), None), P(("rep", "exp"), None, None)),
        check_vma=False,
    )
```

```python
import math

import jax
import jax.numpy as jnp
from jax import lax
from jax.experimental import pallas as pl
from jax.experimental.pallas import tpu as pltpu
from jax.sharding import PartitionSpec as P

ROPE = 64
NOPE = 128


route_scale = 2.827


EXTRA = 128


def other_z(z, dz):
    return (z, z + 1 - 2 * (z % 2), z + 2 - 4 * (z // 2), 3 - z)[dz]


def expert_kernel(
    lengths_ref,
    own_ref,
    gate_up_hbm,
    down_hbm,
    query_latent_hbm,
    query_rope_hbm,
    cache_latent_hbm,
    cache_rope_hbm,
    out_ref,
    attn_ref,
    rows_ref,
    gate_up_ref,
    down_ref,
    part_ref,
    from_core,
    from_q,
    from_p,
    from_z,
    acc,
    select,
    query_latent,
    query_rope,
    cache_latent,
    cache_rope,
    weight_sem,
    attn_sem,
    ag_send,
    ag_recv,
    rs_send,
    rs_recv,
):
    width = down_ref.shape[1]
    tile = 1024
    experts = 16
    me = lax.axis_index("exp")
    core, x, y, z = me % 2, (me // 2) % 2, (me // 4) % 2, me // 8
    p_step, q_step = 4 - 2 * core, 2 + 2 * core
    p_at = y * (1 - core) + x * core
    q_at = x * (1 - core) + y * core

    def device(zz, p, q, c):
        return 8 * zz + p_step * p + q_step * q + c

    sibling = device(z, p_at, q_at, 1 - core)
    p_near = device(z, 1 - p_at, q_at, core)
    q_near = device(z, p_at, 1 - q_at, core)
    z_near = [device(other_z(z, dz), p_at, q_at, core) for dz in range(4)]

    barrier = pltpu.get_barrier_semaphore()
    for partner in (sibling, p_near, q_near, *z_near[1:]):
        pl.semaphore_signal(
            barrier, inc=1, device_id={"exp": partner}, device_id_type=pl.DeviceIdType.MESH
        )
    attn_copies = [
        pltpu.make_async_copy(src, dst, attn_sem.at[i])
        for i, (src, dst) in enumerate(
            (
                (query_latent_hbm, query_latent),
                (query_rope_hbm, query_rope),
                (cache_latent_hbm, cache_latent),
                (cache_rope_hbm, cache_rope),
            )
        )
    ]
    for copy in attn_copies:
        copy.start()
    gate_up_copy = pltpu.make_async_copy(
        gate_up_hbm.reshape(gate_up_ref.shape), gate_up_ref, weight_sem.at[0]
    )
    down_copy = pltpu.make_async_copy(down_hbm, down_ref, weight_sem.at[1])
    gate_up_copy.start()
    down_copy.start()
    rows_ref[me] = own_ref[...]
    pl.semaphore_wait(barrier, 6)

    sent = []

    def remote(src, dst, send, recv, target):
        return pltpu.make_async_remote_copy(
            src_ref=src,
            dst_ref=dst,
            send_sem=send,
            recv_sem=recv,
            device_id={"exp": target},
            device_id_type=pl.DeviceIdType.MESH,
        )

    ag_count = [0]

    def give(block, target):
        copy = remote(
            rows_ref.at[block],
            rows_ref.at[block],
            ag_send.at[ag_count[0]],
            ag_recv.at[block],
            target,
        )
        ag_count[0] += 1
        copy.start()
        sent.append(copy)

    def take(block):
        remote(
            rows_ref.at[block], rows_ref.at[block], ag_send.at[0], ag_recv.at[block], sibling
        ).wait_recv()

    def gather_first(dz):
        zz = other_z(z, dz)
        block = device(zz, p_at, q_at, core)
        if dz == 0:
            for far in (1, 2, 3):
                give(block, z_near[far])
        else:
            take(block)
        give(block, q_near)
        give(block, p_near)
        give(block, sibling)

    def gather_second(dz):
        zz = other_z(z, dz)
        block = device(zz, 1 - p_at, q_at, core)
        take(block)
        give(block, q_near)
        give(block, sibling)

    def gather_last(dz):
        zz = other_z(z, dz)
        for p in (p_at, 1 - p_at):
            block = device(zz, p, 1 - q_at, core)
            take(block)
            give(block, sibling)
        for p in (0, 1):
            for q in (0, 1):
                take(device(zz, p, q, 1 - core))

    rs_count = [0]

    def hand_over(block, slots, slot, recv, target):
        copy = remote(
            part_ref.at[block], slots.at[slot], rs_send.at[rs_count[0]], rs_recv.at[recv], target
        )
        rs_count[0] += 1
        copy.start()
        sent.append(copy)

    def receive(slots, slot, recv):
        remote(
            slots.at[slot], slots.at[slot], rs_send.at[0], rs_recv.at[recv], sibling
        ).wait_recv()

    def add(block, slots, slot):
        total = part_ref[block].astype(jnp.float32) + slots[slot].astype(jnp.float32)
        part_ref[block] = total.astype(jnp.bfloat16)

    def compute(dz):
        zz = other_z(z, dz)
        acc[...] = jnp.zeros_like(acc)
        dims = (((1,), (1,)), ((), ()))
        planes = pl.ds(8 * zz, 8)

        @pl.loop(0, width // tile)
        def _(step):
            columns = pl.ds(pl.multiple_of(step * tile, tile), tile)
            rows = rows_ref[planes, :, columns].reshape(128, tile)
            acc[...] += lax.dot_general(
                rows, gate_up_ref[:, columns], dims, preferred_element_type=jnp.float32
            )

        gate = acc[...]
        up = pltpu.roll(gate, gate.shape[1] - 1, 1)
        even = lax.broadcasted_iota(jnp.int32, gate.shape, 1) % 2 == 0
        spread = jnp.where(even, gate / (1.0 + jnp.exp(-gate)) * up, 0.0).astype(jnp.bfloat16)
        act = jnp.dot(spread, select[...], preferred_element_type=jnp.float32)
        act = act.astype(jnp.bfloat16)
        extra = rows_ref[planes, :, width:].reshape(128, EXTRA).astype(jnp.float32)
        lane = lax.broadcasted_iota(jnp.int32, (128, EXTRA), 1)
        own = (lane == me // 2) | (lane == experts + me // 2)
        mixing = jnp.sum(jnp.where(own, extra, 0.0), axis=1, keepdims=True)

        if dz == 0:
            down_copy.wait()

        @pl.loop(0, width // tile)
        def _(step):
            columns = pl.ds(pl.multiple_of(step * tile, tile), tile)
            result = jnp.dot(act, down_ref[:, columns], preferred_element_type=jnp.float32)
            part_ref[planes, :, columns] = (
                (result * mixing).astype(jnp.bfloat16).reshape(8, 16, tile)
            )

        for yy in (0, 1):
            for xx in (0, 1):
                block = 8 * zz + 4 * yy + 2 * xx + 1 - core
                slot = 4 * dz + 2 * yy + xx
                hand_over(block, from_core, slot, slot, sibling)

    def sum_cores(dz):
        zz = other_z(z, dz)
        for q in (1 - q_at, q_at):
            for i, p in enumerate((1 - p_at, p_at)):
                slot = 4 * dz + (p_step // 2) * p + (q_step // 2) * q
                block = device(zz, p, q, core)
                receive(from_core, slot, slot)
                add(block, from_core, slot)
                if q is not q_at:
                    hand_over(block, from_q, 2 * dz + i, 16 + 2 * dz + i, q_near)

    def sum_q(dz):
        zz = other_z(z, dz)
        for i, p in enumerate((1 - p_at, p_at)):
            block = device(zz, p, q_at, core)
            receive(from_q, 2 * dz + i, 16 + 2 * dz + i)
            add(block, from_q, 2 * dz + i)
            if i == 0:
                hand_over(block, from_p, dz, 24 + dz, p_near)

    def sum_p(dz):
        block = z_near[dz]
        receive(from_p, dz, 24 + dz)
        add(block, from_p, dz)
        if dz:
            hand_over(block, from_z, dz - 1, 27 + dz, z_near[dz])

    def attend(first, last):
        for row in range(first, last):
            keys = cache_latent[row]
            scores = lax.dot_general(
                query_latent[row],
                keys,
                (((1,), (1,)), ((), ())),
                preferred_element_type=jnp.float32,
            )
            scores += jnp.dot(
                query_rope[row], cache_rope[row], preferred_element_type=jnp.float32
            )
            scores *= 1.0 / math.sqrt(NOPE + ROPE)
            live = lax.broadcasted_iota(jnp.int32, scores.shape, 1) < lengths_ref[row]
            scores = jnp.where(live, scores, -1e30)
            top = jnp.max(scores, axis=1, keepdims=True)
            raw = jnp.where(live, jnp.exp(scores - top), 0.0)
            probs = (raw / jnp.sum(raw, axis=1, keepdims=True)).astype(jnp.bfloat16)
            attn_ref[row] = jnp.dot(probs, keys, preferred_element_type=jnp.float32).astype(
                jnp.bfloat16
            )

    quarter = attn_ref.shape[0] // 4
    gather_first(0)
    wide = lax.broadcasted_iota(jnp.int32, select.shape, 0)
    narrow = lax.broadcasted_iota(jnp.int32, select.shape, 1)
    select[...] = jnp.where(wide == 2 * narrow, 1.0, 0.0).astype(jnp.bfloat16)
    for copy in attn_copies:
        copy.wait()
    attend(0, quarter)
    gather_first(1)
    gather_second(0)
    attend(quarter, 2 * quarter)
    gather_first(2)
    gather_second(1)
    gather_last(0)
    gate_up_copy.wait()
    compute(0)
    gather_first(3)
    gather_second(2)
    gather_last(1)
    sum_cores(0)
    compute(1)
    gather_second(3)
    gather_last(2)
    sum_cores(1)
    sum_q(0)
    compute(2)
    gather_last(3)
    sum_cores(2)
    sum_q(1)
    sum_p(0)
    compute(3)
    attend(2 * quarter, 3 * quarter)
    sum_cores(3)
    sum_q(2)
    sum_p(1)
    attend(3 * quarter, 4 * quarter)
    sum_q(3)
    sum_p(2)
    sum_p(3)
    total = part_ref[me].astype(jnp.float32)
    for dz in (1, 2, 3):
        receive(from_z, dz - 1, 27 + dz)
        total = total + from_z[dz - 1].astype(jnp.float32)
    out_ref[...] = total.astype(jnp.bfloat16)
    for copy in sent:
        copy.wait_send()


def experts_layer(lengths, own, gate_up, down, *attention):
    hidden_dev, width = down.shape
    rows_dev = own.shape[0]
    groups = lax.axis_size("exp")
    block = (rows_dev, width)
    flops = 2 * groups * rows_dev * width * hidden_dev * 3
    return pl.pallas_call(
        expert_kernel,
        out_shape=(
            jax.ShapeDtypeStruct(block, jnp.bfloat16),
            jax.ShapeDtypeStruct(attention[0].shape, jnp.bfloat16),
        ),
        in_specs=[
            pl.BlockSpec(memory_space=pltpu.SMEM),
            pl.BlockSpec(memory_space=pltpu.VMEM),
            *([pl.BlockSpec(memory_space=pl.ANY)] * 6),
        ],
        out_specs=(
            pl.BlockSpec(memory_space=pltpu.VMEM),
            pl.BlockSpec(memory_space=pltpu.VMEM),
        ),
        scratch_shapes=[
            pltpu.VMEM((groups, rows_dev, width + EXTRA), jnp.bfloat16),
            pltpu.VMEM((2 * hidden_dev, width), jnp.bfloat16),
            pltpu.VMEM((hidden_dev, width), jnp.bfloat16),
            pltpu.VMEM((groups, *block), jnp.bfloat16),
            pltpu.VMEM((16, *block), jnp.bfloat16),
            pltpu.VMEM((8, *block), jnp.bfloat16),
            pltpu.VMEM((4, *block), jnp.bfloat16),
            pltpu.VMEM((3, *block), jnp.bfloat16),
            pltpu.VMEM((8 * rows_dev, 2 * hidden_dev), jnp.float32),
            pltpu.VMEM((2 * hidden_dev, hidden_dev), jnp.bfloat16),
            *[pltpu.VMEM(array.shape, array.dtype) for array in attention],
            pltpu.SemaphoreType.DMA((2,)),
            pltpu.SemaphoreType.DMA((4,)),
            pltpu.SemaphoreType.DMA((31,)),
            pltpu.SemaphoreType.DMA((groups,)),
            pltpu.SemaphoreType.DMA((31,)),
            pltpu.SemaphoreType.DMA((31,)),
        ],
        compiler_params=pltpu.CompilerParams(
            collective_id=0, has_side_effects=True, vmem_limit_bytes=60 * 2**20
        ),
        cost_estimate=pl.CostEstimate(
            flops=flops, bytes_accessed=6 * hidden_dev * width, transcendentals=0
        ),
    )(lengths, own, gate_up, down, *attention)


def on_device(
    hidden,
    expert_ids,
    router,
    gate_up,
    down_weight,
    query_latent,
    query_rope,
    cache_latent,
    cache_rope,
    lengths,
):
    groups = lax.axis_size("exp")
    experts = groups // 2
    full_gate_up, full_down = (
        lax.all_gather(gate_up, "rep", axis=1, tiled=True),
        lax.all_gather(down_weight, "rep", axis=1, tiled=True),
    )
    slice_gate_up = full_gate_up[0]
    slice_down = full_down[0]
    logits = jnp.dot(hidden, router, preferred_element_type=jnp.float32)
    onehot = (expert_ids[:, :, None] == jnp.arange(experts, dtype=jnp.int32)[None, None, :]).astype(
        jnp.float32
    )
    picked = jnp.sum(onehot * logits[:, None, :], axis=2)
    sigmoid_scores = jax.nn.sigmoid(picked)
    mixing = sigmoid_scores / jnp.sum(sigmoid_scores, axis=1, keepdims=True) * route_scale
    dense_mixing = jnp.sum(onehot * mixing[:, :, None], axis=1)
    high = lax.reduce_precision(dense_mixing, 8, 7)
    extra = jnp.concatenate((high, dense_mixing - high), axis=1)
    extra = jnp.pad(extra, ((0, 0), (0, EXTRA - extra.shape[1]))).astype(jnp.bfloat16)
    own = jnp.concatenate((hidden, extra), axis=1)
    moe_out, attn_latent = experts_layer(
        lengths,
        own,
        slice_gate_up,
        slice_down,
        query_latent,
        query_rope,
        cache_latent,
        cache_rope,
    )
    return (moe_out, attn_latent)


def solution(mesh):
    return jax.shard_map(
        on_device,
        mesh=mesh,
        in_specs=(
            P(("rep", "exp"), None),
            P(("rep", "exp"), None),
            P(),
            P("exp", "rep", None, None),
            P("exp", "rep", None),
            P(("rep", "exp"), None, None),
            P(("rep", "exp"), None, None),
            P(("rep", "exp"), None, None),
            P(("rep", "exp"), None, None),
            P(("rep", "exp")),
        ),
        out_specs=(P(("rep", "exp"), None), P(("rep", "exp"), None, None)),
        check_vma=False,
    )
```

```python
import math

import jax
import jax.numpy as jnp
from jax import lax
from jax.experimental import pallas as pl
from jax.experimental.pallas import tpu as pltpu
from jax.sharding import PartitionSpec as P

ROPE = 64
NOPE = 128


route_scale = 2.827


EXTRA = 128


def other_z(z, dz):
    return (z, z + 1 - 2 * (z % 2), z + 2 - 4 * (z // 2), 3 - z)[dz]


def expert_kernel(
    lengths_ref,
    own_ref,
    gate_up_hbm,
    down_hbm,
    query_latent_hbm,
    query_rope_hbm,
    cache_latent_hbm,
    cache_rope_hbm,
    out_ref,
    attn_ref,
    rows_ref,
    gate_up_ref,
    down_ref,
    part_ref,
    from_core,
    from_q,
    from_p,
    from_z,
    acc,
    act_ref,
    select,
    query_latent,
    query_rope,
    cache_latent,
    cache_rope,
    weight_sem,
    attn_sem,
    ag_send,
    ag_recv,
    rs_send,
    rs_recv,
):
    width = down_ref.shape[1]
    tile = 1024
    experts = 16
    me = lax.axis_index("exp")
    core, x, y, z = me % 2, (me // 2) % 2, (me // 4) % 2, me // 8
    p_step, q_step = 4 - 2 * core, 2 + 2 * core
    p_at = y * (1 - core) + x * core
    q_at = x * (1 - core) + y * core

    def device(zz, p, q, c):
        return 8 * zz + p_step * p + q_step * q + c

    sibling = device(z, p_at, q_at, 1 - core)
    p_near = device(z, 1 - p_at, q_at, core)
    q_near = device(z, p_at, 1 - q_at, core)
    z_near = [device(other_z(z, dz), p_at, q_at, core) for dz in range(4)]

    barrier = pltpu.get_barrier_semaphore()
    for partner in (sibling, p_near, q_near, *z_near[1:]):
        pl.semaphore_signal(
            barrier, inc=1, device_id={"exp": partner}, device_id_type=pl.DeviceIdType.MESH
        )
    attn_copies = [
        pltpu.make_async_copy(src, dst, attn_sem.at[i])
        for i, (src, dst) in enumerate(
            (
                (query_latent_hbm, query_latent),
                (query_rope_hbm, query_rope),
                (cache_latent_hbm, cache_latent),
                (cache_rope_hbm, cache_rope),
            )
        )
    ]
    for copy in attn_copies:
        copy.start()
    gate_up_copy = pltpu.make_async_copy(
        gate_up_hbm.reshape(gate_up_ref.shape), gate_up_ref, weight_sem.at[0]
    )
    down_copy = pltpu.make_async_copy(down_hbm, down_ref, weight_sem.at[1])
    gate_up_copy.start()
    down_copy.start()
    rows_ref[me] = own_ref[...]
    pl.semaphore_wait(barrier, 6)

    sent = []

    def remote(src, dst, send, recv, target):
        return pltpu.make_async_remote_copy(
            src_ref=src,
            dst_ref=dst,
            send_sem=send,
            recv_sem=recv,
            device_id={"exp": target},
            device_id_type=pl.DeviceIdType.MESH,
        )

    ag_count = [0]

    def give(block, target):
        copy = remote(
            rows_ref.at[block],
            rows_ref.at[block],
            ag_send.at[ag_count[0]],
            ag_recv.at[block],
            target,
        )
        ag_count[0] += 1
        copy.start()
        sent.append(copy)

    def take(block):
        remote(
            rows_ref.at[block], rows_ref.at[block], ag_send.at[0], ag_recv.at[block], sibling
        ).wait_recv()

    def gather_first(dz):
        zz = other_z(z, dz)
        block = device(zz, p_at, q_at, core)
        if dz == 0:
            for far in (1, 2, 3):
                give(block, z_near[far])
        else:
            take(block)
        give(block, q_near)
        give(block, p_near)
        give(block, sibling)

    def gather_second(dz):
        zz = other_z(z, dz)
        block = device(zz, 1 - p_at, q_at, core)
        take(block)
        give(block, q_near)
        give(block, sibling)

    def gather_last(dz):
        zz = other_z(z, dz)
        for p in (p_at, 1 - p_at):
            block = device(zz, p, 1 - q_at, core)
            take(block)
            give(block, sibling)
        for p in (0, 1):
            for q in (0, 1):
                take(device(zz, p, q, 1 - core))

    rs_count = [0]

    def hand_over(block, slots, slot, recv, target):
        copy = remote(
            part_ref.at[block], slots.at[slot], rs_send.at[rs_count[0]], rs_recv.at[recv], target
        )
        rs_count[0] += 1
        copy.start()
        sent.append(copy)

    def receive(slots, slot, recv):
        remote(
            slots.at[slot], slots.at[slot], rs_send.at[0], rs_recv.at[recv], sibling
        ).wait_recv()

    def add(block, slots, slot):
        total = part_ref[block].astype(jnp.float32) + slots[slot].astype(jnp.float32)
        part_ref[block] = total.astype(jnp.bfloat16)

    def hidden_units(pair):
        half = z // 2 if pair == 0 else 1 - z // 2
        planes = pl.ds(16 * half, 16)
        acc[...] = jnp.zeros_like(acc)
        dims = (((1,), (1,)), ((), ()))

        @pl.loop(0, width // tile)
        def _(step):
            columns = pl.ds(pl.multiple_of(step * tile, tile), tile)
            rows = rows_ref[planes, :, columns].reshape(256, tile)
            acc[...] += lax.dot_general(
                rows, gate_up_ref[:, columns], dims, preferred_element_type=jnp.float32
            )

        gate = acc[...]
        up = pltpu.roll(gate, gate.shape[1] - 1, 1)
        even = lax.broadcasted_iota(jnp.int32, gate.shape, 1) % 2 == 0
        spread = jnp.where(even, gate / (1.0 + jnp.exp(-gate)) * up, 0.0).astype(jnp.bfloat16)
        act = jnp.dot(spread, select[...], preferred_element_type=jnp.float32)
        act_ref[pl.ds(pl.multiple_of(256 * half, 256), 256), :] = act.astype(jnp.bfloat16)

    def outputs(dz):
        zz = other_z(z, dz)
        planes = pl.ds(8 * zz, 8)
        act = act_ref[pl.ds(pl.multiple_of(128 * zz, 128), 128), :]
        extra = rows_ref[planes, :, width:].reshape(128, EXTRA).astype(jnp.float32)
        lane = lax.broadcasted_iota(jnp.int32, (128, EXTRA), 1)
        own = (lane == me // 2) | (lane == experts + me // 2)
        mixing = jnp.sum(jnp.where(own, extra, 0.0), axis=1, keepdims=True)

        if dz == 0:
            down_copy.wait()

        @pl.loop(0, width // tile)
        def _(step):
            columns = pl.ds(pl.multiple_of(step * tile, tile), tile)
            result = jnp.dot(act, down_ref[:, columns], preferred_element_type=jnp.float32)
            part_ref[planes, :, columns] = (
                (result * mixing).astype(jnp.bfloat16).reshape(8, 16, tile)
            )

        for yy in (0, 1):
            for xx in (0, 1):
                block = 8 * zz + 4 * yy + 2 * xx + 1 - core
                slot = 4 * dz + 2 * yy + xx
                hand_over(block, from_core, slot, slot, sibling)

    def sum_cores(dz):
        zz = other_z(z, dz)
        for q in (1 - q_at, q_at):
            for i, p in enumerate((1 - p_at, p_at)):
                slot = 4 * dz + (p_step // 2) * p + (q_step // 2) * q
                block = device(zz, p, q, core)
                receive(from_core, slot, slot)
                add(block, from_core, slot)
                if q is not q_at:
                    hand_over(block, from_q, 2 * dz + i, 16 + 2 * dz + i, q_near)

    def sum_q(dz):
        zz = other_z(z, dz)
        for i, p in enumerate((1 - p_at, p_at)):
            block = device(zz, p, q_at, core)
            receive(from_q, 2 * dz + i, 16 + 2 * dz + i)
            add(block, from_q, 2 * dz + i)
            if i == 0:
                hand_over(block, from_p, dz, 24 + dz, p_near)

    def sum_p(dz):
        block = z_near[dz]
        receive(from_p, dz, 24 + dz)
        add(block, from_p, dz)
        if dz:
            hand_over(block, from_z, dz - 1, 27 + dz, z_near[dz])

    def attend(first, last):
        for row in range(first, last):
            keys = cache_latent[row]
            scores = lax.dot_general(
                query_latent[row],
                keys,
                (((1,), (1,)), ((), ())),
                preferred_element_type=jnp.float32,
            )
            scores += jnp.dot(
                query_rope[row], cache_rope[row], preferred_element_type=jnp.float32
            )
            scores *= 1.0 / math.sqrt(NOPE + ROPE)
            live = lax.broadcasted_iota(jnp.int32, scores.shape, 1) < lengths_ref[row]
            scores = jnp.where(live, scores, -1e30)
            top = jnp.max(scores, axis=1, keepdims=True)
            raw = jnp.where(live, jnp.exp(scores - top), 0.0)
            probs = (raw / jnp.sum(raw, axis=1, keepdims=True)).astype(jnp.bfloat16)
            attn_ref[row] = jnp.dot(probs, keys, preferred_element_type=jnp.float32).astype(
                jnp.bfloat16
            )

    quarter = attn_ref.shape[0] // 4
    gather_first(0)
    wide = lax.broadcasted_iota(jnp.int32, select.shape, 0)
    narrow = lax.broadcasted_iota(jnp.int32, select.shape, 1)
    select[...] = jnp.where(wide == 2 * narrow, 1.0, 0.0).astype(jnp.bfloat16)
    for copy in attn_copies:
        copy.wait()
    attend(0, quarter)
    gather_first(1)
    gather_second(0)
    attend(quarter, 2 * quarter)
    gather_first(2)
    gather_second(1)
    gather_last(0)
    gather_first(3)
    gather_second(2)
    attend(2 * quarter, 3 * quarter)
    gather_last(1)
    gather_second(3)
    gate_up_copy.wait()
    hidden_units(0)
    outputs(0)
    gather_last(2)
    outputs(1)
    sum_cores(0)
    gather_last(3)
    hidden_units(1)
    sum_cores(1)
    sum_q(0)
    outputs(2)
    sum_q(1)
    sum_p(0)
    outputs(3)
    sum_cores(2)
    sum_p(1)
    attend(3 * quarter, 4 * quarter)
    sum_cores(3)
    sum_q(2)
    sum_q(3)
    sum_p(2)
    sum_p(3)
    total = part_ref[me].astype(jnp.float32)
    for dz in (1, 2, 3):
        receive(from_z, dz - 1, 27 + dz)
        total = total + from_z[dz - 1].astype(jnp.float32)
    out_ref[...] = total.astype(jnp.bfloat16)
    for copy in sent:
        copy.wait_send()


def experts_layer(lengths, own, gate_up, down, *attention):
    hidden_dev, width = down.shape
    rows_dev = own.shape[0]
    groups = lax.axis_size("exp")
    block = (rows_dev, width)
    flops = 2 * groups * rows_dev * width * hidden_dev * 3
    return pl.pallas_call(
        expert_kernel,
        out_shape=(
            jax.ShapeDtypeStruct(block, jnp.bfloat16),
            jax.ShapeDtypeStruct(attention[0].shape, jnp.bfloat16),
        ),
        in_specs=[
            pl.BlockSpec(memory_space=pltpu.SMEM),
            pl.BlockSpec(memory_space=pltpu.VMEM),
            *([pl.BlockSpec(memory_space=pl.ANY)] * 6),
        ],
        out_specs=(
            pl.BlockSpec(memory_space=pltpu.VMEM),
            pl.BlockSpec(memory_space=pltpu.VMEM),
        ),
        scratch_shapes=[
            pltpu.VMEM((groups, rows_dev, width + EXTRA), jnp.bfloat16),
            pltpu.VMEM((2 * hidden_dev, width), jnp.bfloat16),
            pltpu.VMEM((hidden_dev, width), jnp.bfloat16),
            pltpu.VMEM((groups, *block), jnp.bfloat16),
            pltpu.VMEM((16, *block), jnp.bfloat16),
            pltpu.VMEM((8, *block), jnp.bfloat16),
            pltpu.VMEM((4, *block), jnp.bfloat16),
            pltpu.VMEM((3, *block), jnp.bfloat16),
            pltpu.VMEM((16 * rows_dev, 2 * hidden_dev), jnp.float32),
            pltpu.VMEM((groups * rows_dev, hidden_dev), jnp.bfloat16),
            pltpu.VMEM((2 * hidden_dev, hidden_dev), jnp.bfloat16),
            *[pltpu.VMEM(array.shape, array.dtype) for array in attention],
            pltpu.SemaphoreType.DMA((2,)),
            pltpu.SemaphoreType.DMA((4,)),
            pltpu.SemaphoreType.DMA((31,)),
            pltpu.SemaphoreType.DMA((groups,)),
            pltpu.SemaphoreType.DMA((31,)),
            pltpu.SemaphoreType.DMA((31,)),
        ],
        compiler_params=pltpu.CompilerParams(
            collective_id=0, has_side_effects=True, vmem_limit_bytes=60 * 2**20
        ),
        cost_estimate=pl.CostEstimate(
            flops=flops, bytes_accessed=6 * hidden_dev * width, transcendentals=0
        ),
    )(lengths, own, gate_up, down, *attention)


def on_device(
    hidden,
    expert_ids,
    router,
    gate_up,
    down_weight,
    query_latent,
    query_rope,
    cache_latent,
    cache_rope,
    lengths,
):
    groups = lax.axis_size("exp")
    experts = groups // 2
    full_gate_up, full_down = (
        lax.all_gather(gate_up, "rep", axis=1, tiled=True),
        lax.all_gather(down_weight, "rep", axis=1, tiled=True),
    )
    slice_gate_up = full_gate_up[0]
    slice_down = full_down[0]
    logits = jnp.dot(hidden, router, preferred_element_type=jnp.float32)
    onehot = (expert_ids[:, :, None] == jnp.arange(experts, dtype=jnp.int32)[None, None, :]).astype(
        jnp.float32
    )
    picked = jnp.sum(onehot * logits[:, None, :], axis=2)
    sigmoid_scores = jax.nn.sigmoid(picked)
    mixing = sigmoid_scores / jnp.sum(sigmoid_scores, axis=1, keepdims=True) * route_scale
    dense_mixing = jnp.sum(onehot * mixing[:, :, None], axis=1)
    high = lax.reduce_precision(dense_mixing, 8, 7)
    extra = jnp.concatenate((high, dense_mixing - high), axis=1)
    extra = jnp.pad(extra, ((0, 0), (0, EXTRA - extra.shape[1]))).astype(jnp.bfloat16)
    own = jnp.concatenate((hidden, extra), axis=1)
    moe_out, attn_latent = experts_layer(
        lengths,
        own,
        slice_gate_up,
        slice_down,
        query_latent,
        query_rope,
        cache_latent,
        cache_rope,
    )
    return (moe_out, attn_latent)


def solution(mesh):
    return jax.shard_map(
        on_device,
        mesh=mesh,
        in_specs=(
            P(("rep", "exp"), None),
            P(("rep", "exp"), None),
            P(),
            P("exp", "rep", None, None),
            P("exp", "rep", None),
            P(("rep", "exp"), None, None),
            P(("rep", "exp"), None, None),
            P(("rep", "exp"), None, None),
            P(("rep", "exp"), None, None),
            P(("rep", "exp")),
        ),
        out_specs=(P(("rep", "exp"), None), P(("rep", "exp"), None, None)),
        check_vma=False,
    )
```

```python
import math

import jax
import jax.numpy as jnp
from jax import lax
from jax.experimental import pallas as pl
from jax.experimental.pallas import tpu as pltpu
from jax.sharding import PartitionSpec as P

ROPE = 64
NOPE = 128


route_scale = 2.827


EXTRA = 128


def other_z(z, dz):
    return (z, z + 1 - 2 * (z % 2), z + 2 - 4 * (z // 2), 3 - z)[dz]


def expert_kernel(
    lengths_ref,
    own_ref,
    gate_up_hbm,
    down_hbm,
    query_latent_hbm,
    query_rope_hbm,
    cache_latent_hbm,
    cache_rope_hbm,
    out_ref,
    attn_ref,
    rows_ref,
    gate_up_ref,
    down_ref,
    part_ref,
    from_core,
    from_q,
    from_p,
    from_z,
    acc,
    select,
    query_latent,
    query_rope,
    cache_latent,
    cache_rope,
    weight_sem,
    attn_sem,
    ag_send,
    ag_recv,
    rs_send,
    rs_recv,
):
    width = down_ref.shape[1]
    tile = 1024
    experts = 16
    me = lax.axis_index("exp")
    core, x, y, z = me % 2, (me // 2) % 2, (me // 4) % 2, me // 8
    p_step, q_step = 4 - 2 * core, 2 + 2 * core
    p_at = y * (1 - core) + x * core
    q_at = x * (1 - core) + y * core

    def device(zz, p, q, c):
        return 8 * zz + p_step * p + q_step * q + c

    sibling = device(z, p_at, q_at, 1 - core)
    p_near = device(z, 1 - p_at, q_at, core)
    q_near = device(z, p_at, 1 - q_at, core)
    z_near = [device(other_z(z, dz), p_at, q_at, core) for dz in range(4)]

    barrier = pltpu.get_barrier_semaphore()
    for partner in (sibling, p_near, q_near, *z_near[1:]):
        pl.semaphore_signal(
            barrier, inc=1, device_id={"exp": partner}, device_id_type=pl.DeviceIdType.MESH
        )
    attn_copies = [
        pltpu.make_async_copy(src, dst, attn_sem.at[i])
        for i, (src, dst) in enumerate(
            (
                (query_latent_hbm, query_latent),
                (query_rope_hbm, query_rope),
                (cache_latent_hbm, cache_latent),
                (cache_rope_hbm, cache_rope),
            )
        )
    ]
    for copy in attn_copies:
        copy.start()
    gate_up_copy = pltpu.make_async_copy(
        gate_up_hbm.reshape(gate_up_ref.shape), gate_up_ref, weight_sem.at[0]
    )
    down_copy = pltpu.make_async_copy(down_hbm, down_ref, weight_sem.at[1])
    gate_up_copy.start()
    down_copy.start()
    rows_ref[me] = own_ref[...]
    pl.semaphore_wait(barrier, 6)

    sent = []

    def remote(src, dst, send, recv, target):
        return pltpu.make_async_remote_copy(
            src_ref=src,
            dst_ref=dst,
            send_sem=send,
            recv_sem=recv,
            device_id={"exp": target},
            device_id_type=pl.DeviceIdType.MESH,
        )

    ag_count = [0]

    def give(block, target):
        copy = remote(
            rows_ref.at[block],
            rows_ref.at[block],
            ag_send.at[ag_count[0]],
            ag_recv.at[block],
            target,
        )
        ag_count[0] += 1
        copy.start()
        sent.append(copy)

    def take(block):
        remote(
            rows_ref.at[block], rows_ref.at[block], ag_send.at[0], ag_recv.at[block], sibling
        ).wait_recv()

    def gather_first(dz):
        zz = other_z(z, dz)
        block = device(zz, p_at, q_at, core)
        if dz == 0:
            for far in (1, 2, 3):
                give(block, z_near[far])
        else:
            take(block)
        give(block, q_near)
        give(block, p_near)
        give(block, sibling)

    def gather_second(dz):
        zz = other_z(z, dz)
        block = device(zz, 1 - p_at, q_at, core)
        take(block)
        give(block, q_near)
        give(block, sibling)

    def gather_last(dz):
        zz = other_z(z, dz)
        for p in (p_at, 1 - p_at):
            block = device(zz, p, 1 - q_at, core)
            take(block)
            give(block, sibling)
        for p in (0, 1):
            for q in (0, 1):
                take(device(zz, p, q, 1 - core))

    rs_count = [0]

    def hand_over(block, slots, slot, recv, target):
        copy = remote(
            part_ref.at[block], slots.at[slot], rs_send.at[rs_count[0]], rs_recv.at[recv], target
        )
        rs_count[0] += 1
        copy.start()
        sent.append(copy)

    def receive(slots, slot, recv):
        remote(
            slots.at[slot], slots.at[slot], rs_send.at[0], rs_recv.at[recv], sibling
        ).wait_recv()

    def add(block, slots, slot):
        total = part_ref[block].astype(jnp.float32) + slots[slot].astype(jnp.float32)
        part_ref[block] = total.astype(jnp.bfloat16)

    def compute(dz):
        zz = other_z(z, dz)
        acc[...] = jnp.zeros_like(acc)
        dims = (((1,), (1,)), ((), ()))
        planes = pl.ds(8 * zz, 8)

        @pl.loop(0, width // tile)
        def _(step):
            columns = pl.ds(pl.multiple_of(step * tile, tile), tile)
            rows = rows_ref[planes, :, columns].reshape(128, tile)
            acc[...] += lax.dot_general(
                rows, gate_up_ref[:, columns], dims, preferred_element_type=jnp.float32
            )

        gate = acc[...]
        up = pltpu.roll(gate, gate.shape[1] - 1, 1)
        even = lax.broadcasted_iota(jnp.int32, gate.shape, 1) % 2 == 0
        spread = jnp.where(even, gate / (1.0 + jnp.exp(-gate)) * up, 0.0).astype(jnp.bfloat16)
        act = jnp.dot(spread, select[...], preferred_element_type=jnp.float32)
        act = act.astype(jnp.bfloat16)
        extra = rows_ref[planes, :, width:].reshape(128, EXTRA).astype(jnp.float32)
        lane = lax.broadcasted_iota(jnp.int32, (128, EXTRA), 1)
        own = (lane == me // 2) | (lane == experts + me // 2)
        mixing = jnp.sum(jnp.where(own, extra, 0.0), axis=1, keepdims=True)

        if dz == 0:
            down_copy.wait()

        @pl.loop(0, width // tile)
        def _(step):
            columns = pl.ds(pl.multiple_of(step * tile, tile), tile)
            result = jnp.dot(act, down_ref[:, columns], preferred_element_type=jnp.float32)
            part_ref[planes, :, columns] = (
                (result * mixing).astype(jnp.bfloat16).reshape(8, 16, tile)
            )

        for yy in (0, 1):
            for xx in (0, 1):
                block = 8 * zz + 4 * yy + 2 * xx + 1 - core
                slot = 4 * dz + 2 * yy + xx
                hand_over(block, from_core, slot, slot, sibling)

    def sum_cores(dz):
        zz = other_z(z, dz)
        for q in (1 - q_at, q_at):
            for i, p in enumerate((1 - p_at, p_at)):
                slot = 4 * dz + (p_step // 2) * p + (q_step // 2) * q
                block = device(zz, p, q, core)
                receive(from_core, slot, slot)
                add(block, from_core, slot)
                if q is not q_at:
                    hand_over(block, from_q, 2 * dz + i, 16 + 2 * dz + i, q_near)

    def sum_q(dz):
        zz = other_z(z, dz)
        for i, p in enumerate((1 - p_at, p_at)):
            block = device(zz, p, q_at, core)
            receive(from_q, 2 * dz + i, 16 + 2 * dz + i)
            add(block, from_q, 2 * dz + i)
            if i == 0:
                hand_over(block, from_p, dz, 24 + dz, p_near)

    def sum_p(dz):
        block = z_near[dz]
        receive(from_p, dz, 24 + dz)
        add(block, from_p, dz)
        if dz:
            hand_over(block, from_z, dz - 1, 27 + dz, z_near[dz])

    def attend(first, last):
        for row in range(first, last):
            keys = cache_latent[row]
            scores = lax.dot_general(
                query_latent[row],
                keys,
                (((1,), (1,)), ((), ())),
                preferred_element_type=jnp.float32,
            )
            scores += jnp.dot(
                query_rope[row], cache_rope[row], preferred_element_type=jnp.float32
            )
            scores *= 1.0 / math.sqrt(NOPE + ROPE)
            live = lax.broadcasted_iota(jnp.int32, scores.shape, 1) < lengths_ref[row]
            scores = jnp.where(live, scores, -1e30)
            top = jnp.max(scores, axis=1, keepdims=True)
            raw = jnp.where(live, jnp.exp(scores - top), 0.0)
            probs = (raw / jnp.sum(raw, axis=1, keepdims=True)).astype(jnp.bfloat16)
            attn_ref[row] = jnp.dot(probs, keys, preferred_element_type=jnp.float32).astype(
                jnp.bfloat16
            )

    quarter = attn_ref.shape[0] // 4
    gather_first(0)
    wide = lax.broadcasted_iota(jnp.int32, select.shape, 0)
    narrow = lax.broadcasted_iota(jnp.int32, select.shape, 1)
    select[...] = jnp.where(wide == 2 * narrow, 1.0, 0.0).astype(jnp.bfloat16)
    for copy in attn_copies:
        copy.wait()
    attend(0, quarter)
    gather_first(1)
    gather_second(0)
    attend(quarter, 2 * quarter)
    gather_first(2)
    gather_second(1)
    gather_last(0)
    gather_first(3)
    gather_second(2)
    gate_up_copy.wait()
    compute(0)
    gather_second(3)
    gather_last(1)
    sum_cores(0)
    compute(1)
    gather_last(2)
    sum_cores(1)
    sum_q(0)
    compute(2)
    gather_last(3)
    sum_cores(2)
    sum_q(1)
    sum_p(0)
    compute(3)
    attend(2 * quarter, 3 * quarter)
    sum_cores(3)
    sum_q(2)
    sum_p(1)
    attend(3 * quarter, 4 * quarter)
    sum_q(3)
    sum_p(2)
    sum_p(3)
    total = part_ref[me].astype(jnp.float32)
    for dz in (1, 2, 3):
        receive(from_z, dz - 1, 27 + dz)
        total = total + from_z[dz - 1].astype(jnp.float32)
    out_ref[...] = total.astype(jnp.bfloat16)
    for copy in sent:
        copy.wait_send()


def experts_layer(lengths, own, gate_up, down, *attention):
    hidden_dev, width = down.shape
    rows_dev = own.shape[0]
    groups = lax.axis_size("exp")
    block = (rows_dev, width)
    flops = 2 * groups * rows_dev * width * hidden_dev * 3
    return pl.pallas_call(
        expert_kernel,
        out_shape=(
            jax.ShapeDtypeStruct(block, jnp.bfloat16),
            jax.ShapeDtypeStruct(attention[0].shape, jnp.bfloat16),
        ),
        in_specs=[
            pl.BlockSpec(memory_space=pltpu.SMEM),
            pl.BlockSpec(memory_space=pltpu.VMEM),
            *([pl.BlockSpec(memory_space=pl.ANY)] * 6),
        ],
        out_specs=(
            pl.BlockSpec(memory_space=pltpu.VMEM),
            pl.BlockSpec(memory_space=pltpu.VMEM),
        ),
        scratch_shapes=[
            pltpu.VMEM((groups, rows_dev, width + EXTRA), jnp.bfloat16),
            pltpu.VMEM((2 * hidden_dev, width), jnp.bfloat16),
            pltpu.VMEM((hidden_dev, width), jnp.bfloat16),
            pltpu.VMEM((groups, *block), jnp.bfloat16),
            pltpu.VMEM((16, *block), jnp.bfloat16),
            pltpu.VMEM((8, *block), jnp.bfloat16),
            pltpu.VMEM((4, *block), jnp.bfloat16),
            pltpu.VMEM((3, *block), jnp.bfloat16),
            pltpu.VMEM((8 * rows_dev, 2 * hidden_dev), jnp.float32),
            pltpu.VMEM((2 * hidden_dev, hidden_dev), jnp.bfloat16),
            *[pltpu.VMEM(array.shape, array.dtype) for array in attention],
            pltpu.SemaphoreType.DMA((2,)),
            pltpu.SemaphoreType.DMA((4,)),
            pltpu.SemaphoreType.DMA((31,)),
            pltpu.SemaphoreType.DMA((groups,)),
            pltpu.SemaphoreType.DMA((31,)),
            pltpu.SemaphoreType.DMA((31,)),
        ],
        compiler_params=pltpu.CompilerParams(
            collective_id=0, has_side_effects=True, vmem_limit_bytes=60 * 2**20
        ),
        cost_estimate=pl.CostEstimate(
            flops=flops, bytes_accessed=6 * hidden_dev * width, transcendentals=0
        ),
    )(lengths, own, gate_up, down, *attention)


def on_device(
    hidden,
    expert_ids,
    router,
    gate_up,
    down_weight,
    query_latent,
    query_rope,
    cache_latent,
    cache_rope,
    lengths,
):
    groups = lax.axis_size("exp")
    experts = groups // 2
    full_gate_up, full_down = (
        lax.all_gather(gate_up, "rep", axis=1, tiled=True),
        lax.all_gather(down_weight, "rep", axis=1, tiled=True),
    )
    slice_gate_up = full_gate_up[0]
    slice_down = full_down[0]
    logits = jnp.dot(hidden, router, preferred_element_type=jnp.float32)
    onehot = (expert_ids[:, :, None] == jnp.arange(experts, dtype=jnp.int32)[None, None, :]).astype(
        jnp.float32
    )
    picked = jnp.sum(onehot * logits[:, None, :], axis=2)
    sigmoid_scores = jax.nn.sigmoid(picked)
    mixing = sigmoid_scores / jnp.sum(sigmoid_scores, axis=1, keepdims=True) * route_scale
    dense_mixing = jnp.sum(onehot * mixing[:, :, None], axis=1)
    high = lax.reduce_precision(dense_mixing, 8, 7)
    extra = jnp.concatenate((high, dense_mixing - high), axis=1)
    extra = jnp.pad(extra, ((0, 0), (0, EXTRA - extra.shape[1]))).astype(jnp.bfloat16)
    own = jnp.concatenate((hidden, extra), axis=1)
    moe_out, attn_latent = experts_layer(
        lengths,
        own,
        slice_gate_up,
        slice_down,
        query_latent,
        query_rope,
        cache_latent,
        cache_rope,
    )
    return (moe_out, attn_latent)


def solution(mesh):
    return jax.shard_map(
        on_device,
        mesh=mesh,
        in_specs=(
            P(("rep", "exp"), None),
            P(("rep", "exp"), None),
            P(),
            P("exp", "rep", None, None),
            P("exp", "rep", None),
            P(("rep", "exp"), None, None),
            P(("rep", "exp"), None, None),
            P(("rep", "exp"), None, None),
            P(("rep", "exp"), None, None),
            P(("rep", "exp")),
        ),
        out_specs=(P(("rep", "exp"), None), P(("rep", "exp"), None, None)),
        check_vma=False,
    )
```
